32 devices in a mesh: vocab: 4 (over z), prange: 4 (over y, x), query: 2 (over core).
Axes of the slice: x: 2, y: 2, z: 4, core: 2. Of those that a mesh axis runs over, the one named last changes fastest.
Arguments:
- term_ids: int32 [4096, 32], P('query'), may hold values from 0 to 32767
- term_weights: bfloat16 [4096, 32], P('query'), may hold values from 0.049804688 to 1
- impact: bfloat16 [32768, 8192], P('vocab', 'prange'), may hold values from 0.0099487305 to 1
- query_rows: bfloat16 [128, 32768], P(('prange', 'query'), 'vocab'), may hold values from -0.3125 to 0.3125
- candidates: int32 [128, 4], P(('prange', 'query')), may hold values from 0 to 63, all different within a row; in each aligned block of 16 rows (0 to 15, 16 to 31, ...) at most 2 rows name the same one
Outputs:
- first_scores: bfloat16 [4, 2048, 4096], P('prange', 'vocab', 'query')
- rescored: float32 [128, 4, 128], P(('prange', 'query'), None, 'vocab')
The draws below stay inside these ranges and needn't reach their ends.
Inputs may be any that keep to these rules, and one draw needn't show every extreme that they name: `candidates`: each row names 4 different blocks. The 16 rows held by one device name any block at most 2 times, and some block exactly 2 times.
All inputs are finite; a program needn't handle non-finite values.
Results may differ from the reference program's by a relative error of at most 0.019.
Values may be sent and summed in bfloat16 or wider, within the bound.
A program may use at most 192 MiB of HBM per device.

```python
import math
import jax
import jax.numpy as jnp
import numpy as np
from jax import lax

VOCAB = 32768
TERMS = 32
PRUNED = 4096
BLOCK = 128
BLOCKS = 64
PASSAGES = 8192
FULL_ROWS_LOCAL = 16
ROWS = 128
CANDS = 4
MOST = 2
N_VOCAB = 4
N_PRANGE = 4


def plant(result, own_key, low, largest):
    extent = result.shape
    spot = [jax.random.randint(jax.random.fold_in(own_key, axis), (), 0, extent[axis]) for axis in range(len(extent))]
    result = result.at[tuple(spot)].set(low)
    longest = extent.index(max(extent))
    spot[longest] = (spot[longest] + 1) % extent[longest]
    return result.at[tuple(spot)].set(largest)


def block_levels(own_key, shape, split, low, top_value):
    def one(position, shards_of):
        draws = jax.random.uniform(jax.random.fold_in(jax.random.fold_in(own_key, 6), position), (shards_of,), jnp.float32, low / len(split), top_value / len(split))
        return jnp.repeat(jnp.exp(draws), shape[position] // shards_of).reshape((-1,) + (1,) * (len(shape) - position - 1))

    loudness = one(*split[0])
    for cut in split[1:]:
        loudness = loudness * one(*cut)
    return loudness


def cumulative_ranks(number_of, skew):
    loads = [(1 << 20) // math.isqrt(grade ** skew) + 1 for grade in range(1, number_of + 1)]
    scale = 1 + sum(loads) // (1 << 30)
    return np.cumsum(np.array([max(1, weight // scale) for weight in loads]))


def skewed_ids(own_key, extent, count, slope):
    listing = cumulative_ranks(count, slope)
    lot = jax.random.randint(jax.random.fold_in(own_key, 1), extent, 0, int(listing[count - 1]))
    grade = jnp.searchsorted(jnp.asarray(listing, jnp.int32), lot, side="right")
    return jax.random.permutation(jax.random.fold_in(own_key, 2), count)[grade].astype(jnp.int32)


def assign_block(key, own, number, rows, amount, top, most, lean):
    order = jax.random.permutation(key, amount)
    packed, usual = load_shares(amount, rows * top, most, lean, True), load_shares(amount, rows * top, most, lean, False)
    places = jnp.arange(amount)

    def named(sizes, turn):
        used = int((sizes > 0).sum())
        fixed = max(1, used // 4)
        moved = fixed + (places - fixed + turn * (used - fixed)) % max(1, amount - fixed)
        return jnp.zeros((amount,), jnp.int32).at[order[jnp.where(places < fixed, places, moved)]].set(jnp.asarray(sizes, jnp.int32))

    sizes = jnp.where(number % 4 == 0, named(packed, number // 4), named(usual, number - number // 4 - 1))
    mixed = jax.random.permutation(jax.random.fold_in(own, 3), amount)
    donor, taker = mixed[0:amount // 2 * 2:2], mixed[1:amount // 2 * 2:2]
    margin = jnp.minimum(sizes[donor] - 1, most - sizes[taker]) // 2
    margin = jnp.where((donor == order[0]) | (taker == order[0]) | (sizes[taker] == 0), 0, jnp.maximum(margin, 0))
    moved = jax.random.randint(jax.random.fold_in(own, 4), (amount // 2,), 0, 1 << 20) % (margin + 1)
    sizes = sizes.at[donor].add(-moved).at[taker].add(moved)
    items = jnp.searchsorted(jnp.cumsum(sizes), jnp.arange(rows * top), side="right").astype(jnp.int32)
    listing = items.reshape(top, rows).T
    listing = listing[jax.random.permutation(jax.random.fold_in(own, 1), rows)]
    turn = jax.random.randint(jax.random.fold_in(own, 2), (rows, 1), 0, top)
    return jnp.take_along_axis(listing, (jnp.arange(top)[None, :] + turn) % top, axis=1)


def load_shares(amount, total, limit, lean, full):
    weights = [(1 << 20) // math.isqrt(standing ** lean) + 1 for standing in range(1, amount + 1)]
    largest = limit if full else min(limit, max(-(-total // amount), total * weights[0] // sum(weights)))
    least = 1 if total - largest >= amount - 1 else 0
    counts, rest = [largest] + [least] * (amount - 1), total - largest - least * (amount - 1)
    while rest > 0:
        free = [i for i in range(1, amount) if counts[i] < largest] or [i for i in range(1, amount) if counts[i] < limit]
        pool, budget = sum([weights[i] for i in free]), rest
        for i in free:
            extra = min(limit - counts[i], max(1, budget * weights[i] // pool), rest)
            counts[i] = counts[i] + extra
            rest = rest - extra
    return np.array(counts)


def scatter_about(key, shape, scale, most, pieces=(), kind=jnp.bfloat16):
    array = jax.random.normal(key, shape, jnp.float32) * scale
    if len(pieces) > 0:
        array = block_levels(key, shape, pieces, -0.22, 0.18) * array
    return jnp.clip(array, min=-most, max=most).astype(kind)


def setup_inputs(seed: int = 0) -> dict:
    arg_keys = jax.random.split(jax.random.key(seed), 6)
    term_ids = plant(skewed_ids(arg_keys[0], (PRUNED, TERMS), VOCAB, 2), jax.random.fold_in(arg_keys[0], 3), 0, VOCAB - 1).astype(jnp.int32)
    term_weights = jnp.clip(jnp.exp(math.log(1.0) - 2.9996462 * jax.random.uniform(arg_keys[1], (PRUNED, TERMS), jnp.float32) ** block_levels(arg_keys[1], (PRUNED, TERMS), ((0, 2),), -0.2, 0.2)), 0.049804688, 1.0).astype(jnp.bfloat16)
    impact = jnp.clip(jnp.exp(math.log(1.0) - 4.61031033 * jax.random.uniform(arg_keys[2], (VOCAB, PASSAGES), jnp.float32) ** block_levels(arg_keys[2], (VOCAB, PASSAGES), ((0, 4), (1, 4)), -0.2, 0.2)), 0.0099487305, 1.0).astype(jnp.bfloat16)
    query_rows = scatter_about(arg_keys[3], (ROWS, VOCAB), 0.02, 0.3125, ((0, 8), (1, 4)))
    candidates_keys = jax.random.split(jax.random.fold_in(arg_keys[4], 1), ROWS // FULL_ROWS_LOCAL)
    candidates_turns = jax.random.permutation(jax.random.fold_in(arg_keys[4], 3), ROWS // FULL_ROWS_LOCAL)
    candidates = jax.vmap(lambda own, number: assign_block(jax.random.fold_in(arg_keys[4], 2), own, number, FULL_ROWS_LOCAL, BLOCKS, CANDS, MOST, 2))(candidates_keys, candidates_turns).reshape((ROWS, CANDS))
    return dict(term_ids=term_ids, term_weights=term_weights, impact=impact, query_rows=query_rows, candidates=candidates)


def first_block(block_ids, block_weights, impact):
    same_term = (block_ids[:, :, None] == block_ids[:, None, :]).astype(jnp.float32)
    summed = jnp.einsum("qkj,qj->qk", same_term, block_weights.astype(jnp.float32), precision=lax.Precision.HIGHEST)
    merged = summed.astype(jnp.bfloat16).astype(jnp.float32) / jnp.sum(same_term, axis=2)
    collected_tiles = impact[block_ids].astype(jnp.float32)
    shard_width = VOCAB // N_VOCAB
    owners = ((block_ids // shard_width)[:, :, None] == jnp.arange(N_VOCAB, dtype=jnp.int32)[None, None, :]).astype(jnp.float32)
    weighted_impacts = merged[:, :, None] * owners
    shard_pieces = jnp.einsum("ljh,ljg->hlg", weighted_impacts, collected_tiles, precision=lax.Precision.HIGHEST)
    return jnp.sum(shard_pieces.astype(jnp.bfloat16).astype(jnp.float32), axis=0).astype(jnp.bfloat16)


def reference(term_ids, term_weights, impact, query_rows, candidates):
    block_rows = math.gcd(64, PRUNED)
    ids_blocks = term_ids.reshape(-1, block_rows, TERMS)
    weight_blocks = term_weights.reshape(-1, block_rows, TERMS)
    scores = lax.map(lambda pair: first_block(pair[0], pair[1], impact), (ids_blocks, weight_blocks))
    first_scores = scores.reshape(PRUNED, PASSAGES).T.reshape(N_PRANGE, PASSAGES // N_PRANGE, PRUNED)
    block_tiles = impact.reshape(VOCAB, BLOCKS, BLOCK)

    def one_query(pair):
        query_weight_row, blocks_row = pair
        picked = block_tiles[:, blocks_row, :].astype(jnp.float32)
        return jnp.einsum("v,vcp->cp", query_weight_row.astype(jnp.float32), picked, precision=lax.Precision.HIGHEST)

    rescored = lax.map(one_query, (query_rows, candidates))
    return (first_scores, rescored)
```

```python
import functools

import jax
import jax.numpy as jnp
from jax import lax
from jax.experimental import pallas as pl
from jax.experimental.pallas import tpu as pltpu
from jax.sharding import PartitionSpec as P

BLOCK = 128
LOW = 256
GROUP = 8
CHUNKS = (2, 2, 4, 4, 4)


def dense_kernel(high_count, high_ref, low_ref, weight_ref, dense_ref):
    columns = high_ref.shape[1]
    rows = high_count * GROUP
    row_codes = lax.broadcasted_iota(jnp.int32, (rows, columns), 0).astype(jnp.float32).astype(jnp.bfloat16)
    low_codes = lax.broadcasted_iota(jnp.int32, (LOW, columns), 0).astype(jnp.float32).astype(jnp.bfloat16)
    zero = jnp.zeros((), jnp.bfloat16)
    one = jnp.ones((), jnp.bfloat16)

    def group_product(g):
        high = high_ref[g : g + 1, :].astype(jnp.bfloat16)
        low = low_ref[g : g + 1, :].astype(jnp.bfloat16)
        weight = weight_ref[g : g + 1, :].astype(jnp.bfloat16)
        weighted = jnp.where(row_codes == high, jnp.broadcast_to(weight, row_codes.shape), zero)
        picked = jnp.where(low_codes == low, one, zero)
        product = lax.dot_general(
            weighted, picked, (((1,), (1,)), ((), ())), preferred_element_type=jnp.float32
        )
        return product.reshape(high_count, GROUP, LOW)

    for pair in range(high_ref.shape[0] // 2):
        both = jnp.concatenate(
            [group_product(2 * pair), group_product(2 * pair + 1)], axis=1
        ).astype(jnp.bfloat16)
        for h in range(high_count):
            dense_ref[pair * 2 * GROUP : (pair + 1) * 2 * GROUP, h * LOW : (h + 1) * LOW] = both[h]


def densify(high, low, weight, shard_width):
    groups, columns = high.shape
    high_count = shard_width // LOW
    step = 8
    spec = pl.BlockSpec((step, columns), lambda i: (i, 0))
    return pl.pallas_call(
        functools.partial(dense_kernel, high_count),
        grid=(groups // step,),
        in_specs=[spec] * 3,
        out_specs=pl.BlockSpec((step * GROUP, shard_width), lambda i: (i, 0)),
        out_shape=jax.ShapeDtypeStruct((groups * GROUP, shard_width), jnp.bfloat16),
        compiler_params=pltpu.CompilerParams(vmem_limit_bytes=24 * 1024 * 1024),
        cost_estimate=pl.CostEstimate(
            flops=2 * groups * columns * LOW * high_count * GROUP,
            bytes_accessed=2 * groups * GROUP * shard_width,
            transcendentals=0,
        ),
    )(high, low, weight)


def local(term_ids, term_weights, impact, query_rows, candidates):
    shard_width, range_width = impact.shape
    query_count, term_count = term_ids.shape
    range_count = lax.axis_size("prange")
    vocab_count = lax.axis_size("vocab")
    resident_blocks = range_width // BLOCK
    high_count = shard_width // LOW

    all_rows = lax.all_gather(query_rows, "prange", axis=0, tiled=True)
    all_candidates = lax.all_gather(candidates, "prange", axis=0, tiled=True)

    local_ids = term_ids - lax.axis_index("vocab") * shard_width
    high = local_ids // LOW
    low = (local_ids % LOW).astype(jnp.float32)
    lane = jnp.arange(query_count, dtype=jnp.int32)[:, None] % GROUP
    high_code = jnp.where((high >= 0) & (high < high_count), high * GROUP + lane, -1)
    group_shape = (query_count // GROUP, GROUP * term_count)
    high_code = high_code.astype(jnp.float32).reshape(group_shape)
    low = low.reshape(group_shape)
    weight = term_weights.astype(jnp.float32).reshape(group_shape)

    pieces = []
    begin = 0
    codes = (high_code, low, weight)
    for share in CHUNKS:
        size = group_shape[0] * share // sum(CHUNKS)
        cut = slice(begin, begin + size)
        begin += size
        dense_query = densify(*(code[cut] for code in codes), shard_width)
        part = lax.dot_general(
            impact, dense_query, (((0,), (1,)), ((), ())), preferred_element_type=jnp.float32
        ).astype(jnp.bfloat16)
        codes, all_rows, part = lax.optimization_barrier((codes, all_rows, part))
        pieces.append(lax.psum_scatter(part, "vocab", scatter_dimension=0, tiled=True))
        if len(pieces) >= 3:
            codes, pieces[-3] = lax.optimization_barrier((codes, pieces[-3]))
        if len(pieces) == 3:
            scores = jnp.dot(all_rows, impact, preferred_element_type=jnp.float32)
            scores = scores.reshape(-1, resident_blocks, BLOCK)
            own = all_candidates - lax.axis_index("prange") * resident_blocks
            chosen = own[:, :, None] == jnp.arange(resident_blocks, dtype=jnp.int32)
            picked = jnp.sum(
                jnp.where(chosen[:, :, :, None], scores[:, None, :, :], 0.0), axis=2
            )
            full_count, cands = candidates.shape
            share_width = BLOCK // vocab_count
            picked = picked.reshape(range_count, full_count * cands, vocab_count, share_width)
            picked = picked.transpose(2, 0, 1, 3).reshape(
                vocab_count * range_count, full_count * cands * share_width
            )
            codes, picked, pieces[0] = lax.optimization_barrier((codes, picked, pieces[0]))
            summed = lax.psum_scatter(
                picked, ("vocab", "prange"), scatter_dimension=0, tiled=True
            )
            rescored = summed.reshape(full_count, cands, share_width)
    first_scores = jnp.concatenate(pieces, axis=1)[None]
    return (first_scores, rescored)


def solution(mesh):
    return jax.shard_map(
        local,
        mesh=mesh,
        in_specs=(
            P("query", None),
            P("query", None),
            P("vocab", "prange"),
            P(("prange", "query"), "vocab"),
            P(("prange", "query"), None),
        ),
        out_specs=(P("prange", "vocab", "query"), P(("prange", "query"), None, "vocab")),
        check_vma=False,
    )
```

```python
import functools

import jax
import jax.numpy as jnp
from jax import lax
from jax.experimental import pallas as pl
from jax.experimental.pallas import tpu as pltpu
from jax.sharding import PartitionSpec as P

BLOCK = 128
LOW = 256
GROUP = 8
CHUNKS = (1, 3, 4)


def dense_kernel(high_count, high_ref, low_ref, weight_ref, dense_ref):
    columns = high_ref.shape[1]
    rows = high_count * GROUP
    row_codes = lax.broadcasted_iota(jnp.int32, (rows, columns), 0).astype(jnp.float32).astype(jnp.bfloat16)
    low_codes = lax.broadcasted_iota(jnp.int32, (LOW, columns), 0).astype(jnp.float32).astype(jnp.bfloat16)
    zero = jnp.zeros((), jnp.bfloat16)
    one = jnp.ones((), jnp.bfloat16)

    def group_product(g):
        high = high_ref[g : g + 1, :].astype(jnp.bfloat16)
        low = low_ref[g : g + 1, :].astype(jnp.bfloat16)
        weight = weight_ref[g : g + 1, :].astype(jnp.bfloat16)
        weighted = jnp.where(row_codes == high, jnp.broadcast_to(weight, row_codes.shape), zero)
        picked = jnp.where(low_codes == low, one, zero)
        product = lax.dot_general(
            weighted, picked, (((1,), (1,)), ((), ())), preferred_element_type=jnp.float32
        )
        return product.reshape(high_count, GROUP, LOW)

    for pair in range(high_ref.shape[0] // 2):
        both = jnp.concatenate(
            [group_product(2 * pair), group_product(2 * pair + 1)], axis=1
        ).astype(jnp.bfloat16)
        for h in range(high_count):
            dense_ref[pair * 2 * GROUP : (pair + 1) * 2 * GROUP, h * LOW : (h + 1) * LOW] = both[h]


def densify(high, low, weight, shard_width):
    groups, columns = high.shape
    high_count = shard_width // LOW
    step = 8
    spec = pl.BlockSpec((step, columns), lambda i: (i, 0))
    return pl.pallas_call(
        functools.partial(dense_kernel, high_count),
        grid=(groups // step,),
        in_specs=[spec] * 3,
        out_specs=pl.BlockSpec((step * GROUP, shard_width), lambda i: (i, 0)),
        out_shape=jax.ShapeDtypeStruct((groups * GROUP, shard_width), jnp.bfloat16),
        compiler_params=pltpu.CompilerParams(vmem_limit_bytes=24 * 1024 * 1024),
        cost_estimate=pl.CostEstimate(
            flops=2 * groups * columns * LOW * high_count * GROUP,
            bytes_accessed=2 * groups * GROUP * shard_width,
            transcendentals=0,
        ),
    )(high, low, weight)


def local(term_ids, term_weights, impact, query_rows, candidates):
    shard_width, range_width = impact.shape
    query_count, term_count = term_ids.shape
    range_count = lax.axis_size("prange")
    vocab_count = lax.axis_size("vocab")
    resident_blocks = range_width // BLOCK
    high_count = shard_width // LOW

    local_ids = term_ids - lax.axis_index("vocab") * shard_width
    high = local_ids // LOW
    low = (local_ids % LOW).astype(jnp.float32)
    lane = jnp.arange(query_count, dtype=jnp.int32)[:, None] % GROUP
    high_code = jnp.where((high >= 0) & (high < high_count), high * GROUP + lane, -1)
    group_shape = (query_count // GROUP, GROUP * term_count)
    high_code = high_code.astype(jnp.float32).reshape(group_shape)
    low = low.reshape(group_shape)
    weight = term_weights.astype(jnp.float32).reshape(group_shape)

    pieces = []
    begin = 0
    codes = (high_code, low, weight)
    for share in CHUNKS:
        size = group_shape[0] * share // sum(CHUNKS)
        cut = slice(begin, begin + size)
        begin += size
        dense_query = densify(*(code[cut] for code in codes), shard_width)
        part = lax.dot_general(
            impact, dense_query, (((0,), (1,)), ((), ())), preferred_element_type=jnp.float32
        ).astype(jnp.bfloat16)
        codes, query_rows, candidates, part = lax.optimization_barrier(
            (codes, query_rows, candidates, part)
        )
        pieces.append(lax.psum_scatter(part, "vocab", scatter_dimension=0, tiled=True))

    full_count, cands = candidates.shape
    all_rows = lax.all_to_all(
        jnp.broadcast_to(query_rows[None], (range_count, full_count, shard_width)),
        "prange", split_axis=0, concat_axis=0, tiled=True,
    ).reshape(range_count * full_count, shard_width)
    all_candidates = lax.all_gather(candidates, "prange", axis=0, tiled=True)
    scores = jnp.dot(all_rows, impact, preferred_element_type=jnp.float32)
    scores = scores.reshape(-1, resident_blocks, BLOCK)
    own = all_candidates - lax.axis_index("prange") * resident_blocks
    chosen = own[:, :, None] == jnp.arange(resident_blocks, dtype=jnp.int32)
    picked = jnp.sum(jnp.where(chosen[:, :, :, None], scores[:, None, :, :], 0.0), axis=2)
    share_width = BLOCK // vocab_count
    picked = picked.reshape(range_count, full_count * cands, vocab_count, share_width)
    picked = picked.transpose(2, 0, 1, 3).reshape(
        vocab_count * range_count, full_count * cands * share_width
    )
    arrived = lax.all_to_all(
        picked, ("vocab", "prange"), split_axis=0, concat_axis=0, tiled=True
    )
    rescored = jnp.sum(arrived, axis=0).reshape(full_count, cands, share_width)
    first_scores = jnp.concatenate(pieces, axis=1)[None]
    return (first_scores, rescored)


def solution(mesh):
    return jax.shard_map(
        local,
        mesh=mesh,
        in_specs=(
            P("query", None),
            P("query", None),
            P("vocab", "prange"),
            P(("prange", "query"), "vocab"),
            P(("prange", "query"), None),
        ),
        out_specs=(P("prange", "vocab", "query"), P(("prange", "query"), None, "vocab")),
        check_vma=False,
    )
```
